512 devices in a mesh: replica: 4 (over z_lo), fsdp: 16 (over y, x), tensor: 8 (over z_hi, core).
Axes of the slice: x: 4, y: 4, z: 16 (z_hi: 4, z_lo: 4; z = z_hi * 4 + z_lo), core: 2. Of those that a mesh axis runs over, the one named last changes fastest.
Arguments:
- inputs: bfloat16 [32768, 8192], P(('replica', 'fsdp'), 'tensor'), may hold values from -0.032958984 to 0.032958984
- kv_grad: bfloat16 [32768, 2048], P(('replica', 'fsdp'), 'tensor'), may hold values from -6 to 6
- weight_blocks: bfloat16 [8, 128, 128, 128], P('tensor', 'fsdp'), may hold values from -0.1875 to 0.1875
- bitmap: int32 [64, 16], P('tensor'), may hold values from 0 to 1, as said below
- counts: int32 [8, 16], P('tensor'), may hold values from 0 to 8, as said below
Outputs:
- input_grad: bfloat16 [32768, 8192], P(('replica', 'fsdp'), 'tensor')
- weight_grad: float32 [8, 128, 128, 128], P('tensor', 'fsdp')
The draws below stay inside these ranges and needn't reach their ends.
Inputs may be any that keep to these rules, and one draw needn't show every extreme that they name: `bitmap`: in every band of 8 rows (rows b * 8 to (b + 1) * 8 - 1) exactly 64 entries are 1. `counts`: each row sums to 64 and its largest entry is 8.
All inputs are finite; a program needn't handle non-finite values.
Results may differ from the reference program's by a relative error of at most 0.001.
Values may be sent and summed in bfloat16 or wider, within the bound.
A program may use at most 64 MiB of HBM per device.

```python
import jax
import jax.numpy as jnp

D = 8192
HD = 128
KVH = 8
BLK = 128
NBR = 64
BANDS = 8
ROWS_DEV = 8
LIVE = 64
CAP = 8
TOKENS = 32768
N_FSDP = 16


def draw_bitmap(key, part):
    key = jax.random.fold_in(key, 5)
    keys = jax.random.split(key, BANDS)

    def one_band(subkey):
        ranking = jax.random.permutation(subkey, ROWS_DEV * 2 * KVH)
        return (ranking < LIVE).astype(jnp.int32).reshape(ROWS_DEV, 2 * KVH)
    bands = jax.vmap(one_band)(keys)
    return bands.reshape(NBR, 2 * KVH)


def draw_counts(key, part):
    key = jax.random.fold_in(key, 9)
    keys = jax.random.split(key, BANDS)
    half_count = N_FSDP // 2
    even_share = LIVE // N_FSDP

    def one_band(subkey):
        first_key, second_key, third_key = jax.random.split(subkey, 3)
        flipped = jax.random.randint(first_key, (), 0, 2)
        places = jnp.arange(N_FSDP, dtype=jnp.int32)
        lower_half = places < half_count
        filled = jnp.where(flipped == 0, lower_half, jnp.logical_not(lower_half))
        base_counts = jnp.where(filled, CAP, 0).astype(jnp.int32)
        moved = jax.random.randint(second_key, (), 0, even_share)
        donor = jnp.where(flipped == 0, 0, N_FSDP - 1)
        taker_local = jax.random.randint(third_key, (), 0, half_count)
        taker = jnp.where(flipped == 0, half_count + taker_local, taker_local)
        result = base_counts - jnp.where(places == donor, moved, 0) + jnp.where(places == taker, moved, 0)
        return result.astype(jnp.int32)
    return jax.vmap(one_band)(keys)


def levels(stream_key, extent, cuts, least, top_value):
    def one(position, shards_of):
        draws = jax.random.uniform(jax.random.fold_in(jax.random.fold_in(stream_key, 6), position), (shards_of,), jnp.float32, least / len(cuts), top_value / len(cuts))
        return jnp.repeat(jnp.exp(draws), extent[position] // shards_of).reshape((-1,) + (1,) * (len(extent) - position - 1))

    loudness = one(*cuts[0])
    for cut in cuts[1:]:
        loudness = loudness * one(*cut)
    return loudness


def centred(own_key, shape, width, bound, pieces=(), held_as=jnp.bfloat16):
    array = width * jax.random.normal(own_key, shape, jnp.float32)
    if pieces:
        array = array * levels(own_key, shape, pieces, -0.22, 0.18)
    return jnp.clip(array, -bound, bound).astype(held_as)


def setup_inputs(seed: int = 0) -> dict:
    key_of = jax.random.split(jax.random.key(seed), 6)
    return {
        "inputs": centred(key_of[0], (TOKENS, D), (TOKENS ** -0.5), 0.032958984, ((0, 64), (1, 8))),
        "kv_grad": centred(key_of[1], (TOKENS, 2 * KVH * HD), 1.0, 6.0, ((0, 64), (1, 8))),
        "weight_blocks": centred(key_of[2], (BANDS, N_FSDP * CAP, BLK, BLK), (HD * KVH) ** -0.5, 0.1875, ((0, 8), (1, 16))),
        "bitmap": draw_bitmap(jax.random.fold_in(key_of[5], 71), 0),
        "counts": draw_counts(jax.random.fold_in(key_of[5], 71), 0),
    }


def block_places(bit_flags, packed):
    ranking = jnp.cumsum(bit_flags) - 1
    matches = (bit_flags[None, :] == 1) & (ranking[None, :] == packed[:, None])
    places = jnp.arange(bit_flags.shape[0], dtype=jnp.int32)
    return jnp.sum(jnp.where(matches, places[None, :], 0), axis=1).astype(jnp.int32)


def reference(inputs, kv_grad, weight_blocks, bitmap, counts):
    col_width = 2 * KVH
    positions = ROWS_DEV * col_width
    slot_ids = jnp.arange(N_FSDP * CAP, dtype=jnp.int32)
    source = slot_ids // CAP
    slot_local = slot_ids - source * CAP
    band_outputs = []
    weight_parts = []
    for band_index in range(BANDS):
        low_row = band_index * ROWS_DEV
        bit_flags = bitmap[low_row:low_row + ROWS_DEV].reshape(-1)
        band_counts = counts[band_index]
        offsets = jnp.cumsum(band_counts) - band_counts
        packed = (offsets[source] + slot_local).astype(jnp.int32)
        is_valid = slot_local < band_counts[source]
        slot_places = block_places(bit_flags, packed)
        target = jnp.where(is_valid, slot_places, positions).astype(jnp.int32)
        dense_blocks = jnp.zeros((positions + 1, BLK, BLK), jnp.float32)
        dense_blocks = dense_blocks.at[target].set(weight_blocks[band_index].astype(jnp.float32))
        dense_blocks = dense_blocks[:positions].reshape(ROWS_DEV, col_width, BLK, BLK)
        matrix = dense_blocks.transpose(0, 2, 1, 3).reshape(ROWS_DEV * BLK, col_width * BLK).astype(jnp.bfloat16)
        band_inputs = inputs[:, low_row * BLK:(low_row + ROWS_DEV) * BLK]
        band_outputs.append(jnp.dot(kv_grad, matrix.T, preferred_element_type=jnp.float32).astype(jnp.bfloat16))
        outer_terms = jnp.dot(band_inputs.T, kv_grad, preferred_element_type=jnp.float32)
        outer_terms = outer_terms.reshape(ROWS_DEV, BLK, col_width, BLK).transpose(0, 2, 1, 3)
        outer_terms = outer_terms.reshape(positions, BLK, BLK)
        picked = outer_terms[jnp.where(is_valid, slot_places, 0).astype(jnp.int32)]
        weight_parts.append(jnp.where(is_valid[:, None, None], picked, jnp.zeros_like(picked)))
    input_grad = jnp.concatenate(band_outputs, axis=1)
    return input_grad, jnp.stack(weight_parts)
```

```python
import functools

import jax
import jax.numpy as jnp
from jax import lax
from jax.experimental import pallas as pl
from jax.experimental.pallas import tpu as pltpu
from jax.sharding import PartitionSpec as P

MESH = pl.DeviceIdType.MESH
RADIUS = 32700.0
STEPS = 16.0
LIFT = 2048.0
PIECES = 4
M_R, M_L, O_R, O_L, C_R, C_L = range(6)


def encode(buf, count, k, block):
    half = block.shape[0] // 2
    peak = jnp.maximum(jnp.max(jnp.abs(block), axis=0, keepdims=True), 1e-30)
    code = (jnp.log(peak) * STEPS + LIFT).astype(jnp.int32) + 1
    scale = jnp.exp((code.astype(jnp.float32) - LIFT) * (1.0 / STEPS))
    whole = jnp.round(block * (RADIUS / scale)).astype(jnp.int32)
    buf[pl.ds(pl.multiple_of(k * half, half), half), :] = whole[:half] * 65536 + whole[half:]
    buf[pl.ds(count * half + k, 1), :] = code


def decode(buf, count, k, side):
    half = side // 2
    pair = buf[pl.ds(pl.multiple_of(k * half, half), half), :]
    code = buf[pl.ds(count * half + k, 1), :]
    scale = jnp.exp((code.astype(jnp.float32) - LIFT) * (1.0 / STEPS)) * (1.0 / RADIUS)
    low = (pair << 16) >> 16
    high = (pair - low) >> 16
    return jnp.concatenate([high.astype(jnp.float32), low.astype(jnp.float32)], axis=0) * scale


def kernel(
    slot_place, place_slot, shard_counts, inputs, kv_grad, weights,
    input_grad, weight_grad,
    x_in, x_turned, kvg, wg, dense, terms, grad_out, part, total,
    send1, recv1, send2, recv2, zsend1, zrecv1, zsend2, zrecv2,
    local_sem, kv_send, kv_recv, w_send, w_recv, rs_send, rs_recv, z_send, z_recv,
):
    rep = lax.axis_index("replica")
    shard = lax.axis_index("fsdp")
    band = lax.axis_index("tensor")
    tokens, width = x_in.shape
    side = terms.shape[-1]
    cap = weights.shape[1]
    cols = kv_grad.shape[1]
    hc = cap // 2
    ring = 4
    rows, groups = width // side, 8
    col_blocks = cols // side * groups
    piece = tokens // PIECES

    def shift(f, axis, by):
        y, x = f // ring, f % ring
        if axis == "x":
            return y * ring + (x + by + ring) % ring
        return ((y + by + ring) % ring) * ring + x

    def near(axis, by):
        return {"fsdp": shift(shard, axis, by)}

    def band_at(by):
        return (band + 2 * by + groups) % groups

    sibling = band + 1 - 2 * (band % 2)

    def sibling_at(by):
        return (sibling + 2 * by + groups) % groups

    def remote(src, dst, send_sem, recv_sem, where):
        return pltpu.make_async_remote_copy(
            src_ref=src, dst_ref=dst, send_sem=send_sem, recv_sem=recv_sem,
            device_id=where, device_id_type=MESH,
        )

    partners = [{"tensor": sibling}, {"tensor": band_at(1)}, {"tensor": band_at(-1)}]
    partners += [near(axis, by) for axis in ("x", "y") for by in (1, -1)]
    partners += [{"replica": (rep + d) % 4} for d in (1, 2, 3)]
    barrier = pltpu.get_barrier_semaphore()
    for where in partners:
        pl.semaphore_signal(barrier, inc=1, device_id=where, device_id_type=MESH)
    pl.semaphore_wait(barrier, len(partners))

    sent = []

    def go(copy):
        copy.start()
        sent.append(copy)

    def kv_at(b, p, n=1):
        return kvg.at[b, pl.ds(p * piece, n * piece), :]

    own_kv = [kv_grad.at[pl.ds(p * piece, piece), :] for p in range(PIECES)]
    right_order = list(range(PIECES))
    left_order = right_order[PIECES // 2:] + right_order[:PIECES // 2]
    for a, b in zip(right_order, left_order):
        go(remote(own_kv[a], kv_at(band, a), kv_send.at[0, a], kv_recv.at[0, a], {"tensor": band_at(1)}))
        go(remote(own_kv[b], kv_at(band, b), kv_send.at[1, b], kv_recv.at[1, b], {"tensor": band_at(-1)}))

    firsts = ("x", "y")
    seconds = ("y", "x")

    def w_at(f, slot, n):
        return wg.at[pl.ds(f * cap + slot, n)]

    for h in range(2):
        own_w = weights.at[0, pl.ds(hc * h, hc)]
        for d, by in ((0, 1), (1, -1)):
            go(remote(own_w, w_at(shard, hc * h, hc), w_send.at[h, 0, d], w_recv.at[h, 0, d], near(firsts[h], by)))
            go(remote(own_w, w_at(shard, hc * h, hc), w_send.at[h, 2, d], w_recv.at[h, 2, d], near(seconds[h], by)))
    go(remote(kv_grad, kv_at(band, 0, PIECES), kv_send.at[3, 0], kv_recv.at[3, 0], {"tensor": sibling}))
    local = [
        pltpu.make_async_copy(inputs, x_in, local_sem.at[0]),
        pltpu.make_async_copy(kv_grad, kvg.at[band], local_sem.at[1]),
        pltpu.make_async_copy(weights.at[0], w_at(shard, 0, cap), local_sem.at[2]),
    ]
    for copy in local:
        copy.start()

    def kv_wait(which, p, b, n=1):
        remote(kv_at(b, p, n), kv_at(b, p, n), kv_send.at[which, p], kv_recv.at[which, p], {"tensor": sibling}).wait_recv()

    def kv_pass(which, p, b):
        go(remote(kv_at(b, p), kv_at(b, p), kv_send.at[which, p], kv_recv.at[which, p], {"tensor": sibling}))

    def kv_relay(p, b, by):
        go(remote(kv_at(b, p), kv_at(b, p), kv_send.at[2, p], kv_recv.at[2, p], {"tensor": band_at(by)}))

    def w_wait(h, which, d, f, slot, n):
        at = w_at(f, hc * h + slot, n)
        remote(at, at, w_send.at[h, which, d], w_recv.at[h, which, d], {"tensor": sibling}).wait_recv()

    def w_go(h, which, d, f, slot, n, axis):
        at = w_at(f, hc * h + slot, n)
        go(remote(at, at, w_send.at[h, which, d], w_recv.at[h, which, d], near(axis, 1 if d == 0 else -1)))

    hq = hc // 2

    def w_first(h):
        for d, by in ((0, -1), (1, 1)):
            src = shift(shard, firsts[h], by)
            w_wait(h, 0, d, src, 0, hc)
            w_go(h, 1, d, src, d * hq, hq, firsts[h])
            for e in range(2):
                w_go(h, 3 + d, e, src, 0, hc, seconds[h])

    def w_far(h):
        src = shift(shard, firsts[h], 2)
        for d in range(2):
            w_wait(h, 1, d, src, d * hq, hq)
        for e in range(2):
            w_go(h, 5, e, src, 0, hc, seconds[h])

    def w_second(h, s):
        for d, by in ((0, -1), (1, 1)):
            src = shift(shift(shard, firsts[h], (0, -1, 1, 2)[s]), seconds[h], by)
            w_wait(h, 2 + s, d, src, 0, hc)
            w_go(h, 6 + s, d, src, d * hq, hq, seconds[h])

    def w_last(h, s):
        src = shift(shift(shard, firsts[h], (0, -1, 1, 2)[s]), seconds[h], 2)
        for d in range(2):
            w_wait(h, 6 + s, d, src, d * hq, hq)

    def outer(b):
        def tile(i, carry):
            at = pl.ds(pl.multiple_of(i * 2 * side, 2 * side), 2 * side)
            got = jnp.dot(x_turned[at, :], kvg[b], preferred_element_type=jnp.float32)
            for u in range(2):
                for v in range(2):
                    place = (2 * i + u) * col_blocks + 2 * b + v
                    terms[place] = got[u * side:(u + 1) * side, v * side:(v + 1) * side]
            return carry

        lax.fori_loop(0, rows // 2, tile, 0)

    local[0].wait()
    local[1].wait()
    x_turned[...] = x_in[...].T
    for h in range(2):
        w_first(h)
    outer(band)
    for p, q in ((0, 2), (1, 3)):
        kv_wait(0, p, band_at(-1))
        kv_relay(p, band_at(-1), 1)
        kv_wait(1, q, band_at(1))
        kv_relay(q, band_at(1), -1)
        kv_pass(4, p, band_at(-1))
        kv_pass(5, q, band_at(1))
        if p == 0:
            for h in range(2):
                w_far(h)
            for h in range(2):
                w_second(h, 0)
            kv_wait(3, 0, sibling, PIECES)
            outer(sibling)
    for s in range(1, 4):
        for h in range(2):
            w_second(h, s)
    for p, q in ((2, 0), (3, 1)):
        kv_wait(0, p, band_at(-1))
        kv_pass(4, p, band_at(-1))
        kv_wait(1, q, band_at(1))
        kv_pass(5, q, band_at(1))
    outer(band_at(-1))
    outer(band_at(1))
    for p in range(PIECES):
        kv_wait(4, p, sibling_at(-1))
        kv_wait(5, p, sibling_at(1))
    outer(sibling_at(-1))
    outer(sibling_at(1))
    for p in (0, 2, 1, 3):
        kv_wait(2, p, band_at(2))
        kv_pass(6, p, band_at(2))
    outer(band_at(2))
    for p in (0, 2, 1, 3):
        kv_wait(6, p, sibling_at(2))
    outer(sibling_at(2))

    def coord(axis):
        return shard % ring if axis == "x" else shard // ring

    def owner(h, one, two):
        return two * ring + one if firsts[h] == "x" else one * ring + two

    def term1(h, one, k, upper):
        slot = owner(h, one, k // hq) * cap + hc * h + upper * hq + k % hq
        return terms[slot_place[slot]]

    n1 = ring * hq
    kinds = {M_R: (2, 0, 1), M_L: (2, 1, -1), O_R: (1, 1, 1), O_L: (-1, 0, -1), C_R: (1, 0, 1), C_L: (-1, 1, -1)}

    def rs_copy(phase, h, kind):
        axis = (firsts if phase == 0 else seconds)[h]
        src, dst = ((send1, recv1), (send2, recv2))[phase]
        return remote(
            src.at[h, kind], dst.at[h, kind], rs_send.at[phase, h, kind], rs_recv.at[phase, h, kind],
            near(axis, kinds[kind][2]),
        )

    def first_send(h, kind):
        by, upper, _ = kinds[kind]
        one = (coord(firsts[h]) + by + ring) % ring
        buf = send1.at[h, kind]
        if kind in (C_R, C_L):
            got = recv1.at[h, M_R if kind == C_R else M_L]
            rs_copy(0, h, M_R if kind == C_R else M_L).wait_recv()

        def block(k, carry):
            value = term1(h, one, k, upper)
            if kind in (C_R, C_L):
                value = value + decode(got, n1, k, side)
            encode(buf, n1, k, value)
            return carry

        lax.fori_loop(0, n1, block, 0)
        go(rs_copy(0, h, kind))

    for kind in (M_R, M_L, O_R, O_L, C_R, C_L):
        for h in range(2):
            first_send(h, kind)

    for h in range(2):
        for s in range(4):
            w_last(h, s)
    local[2].wait()
    wg[wg.shape[0] - 1] = jnp.zeros((side, side), wg.dtype)

    def fill(i, carry):
        for j in range(col_blocks):
            place = i * col_blocks + j
            dense[pl.ds(pl.multiple_of(i * side, side), side), j * side:(j + 1) * side] = wg[place_slot[place]]
        return carry

    lax.fori_loop(0, rows, fill, 0)

    def product(i, carry):
        at = pl.ds(pl.multiple_of(i * 2 * side, 2 * side), 2 * side)
        acc = jnp.zeros((tokens, 2 * side), jnp.float32)
        for b in range(groups):
            acc = acc + lax.dot_general(
                kvg[b], dense[at, b * cols:(b + 1) * cols], (((1,), (1,)), ((), ())),
                preferred_element_type=jnp.float32,
            )
        grad_out[:, at] = acc.astype(grad_out.dtype)
        return carry

    lax.fori_loop(0, rows // 2, product, 0)
    out_copy = pltpu.make_async_copy(grad_out, input_grad, local_sem.at[3])
    out_copy.start()

    for h in range(2):
        for kind in (O_R, O_L, C_R, C_L):
            rs_copy(0, h, kind).wait_recv()
        one = coord(firsts[h])

        def add(k, carry):
            for upper in range(2):
                pair = (C_R, O_L) if upper == 0 else (C_L, O_R)
                value = term1(h, one, k, upper)
                for kind in pair:
                    value = value + decode(recv1.at[h, kind], n1, k, side)
                part[h, (k // hq) * hc + upper * hq + k % hq] = value
            return carry

        lax.fori_loop(0, n1, add, 0)

    def second_send(h, kind):
        by, upper, _ = kinds[kind]
        two = (coord(seconds[h]) + by + ring) % ring
        if kind in (C_R, C_L):
            got = recv2.at[h, M_R if kind == C_R else M_L]
            rs_copy(1, h, M_R if kind == C_R else M_L).wait_recv()
        for k in range(hq):
            value = part[h, two * hc + upper * hq + k]
            if kind in (C_R, C_L):
                value = value + decode(got, hq, k, side)
            encode(send2.at[h, kind], hq, k, value)
        go(rs_copy(1, h, kind))

    for kind in (M_R, M_L, O_R, O_L, C_R, C_L):
        for h in range(2):
            second_send(h, kind)
    for h in range(2):
        two = coord(seconds[h])
        for kind in (O_R, O_L, C_R, C_L):
            rs_copy(1, h, kind).wait_recv()
        for upper in range(2):
            pair = (C_R, O_L) if upper == 0 else (C_L, O_R)
            for k in range(hq):
                value = part[h, two * hc + upper * hq + k]
                for kind in pair:
                    value = value + decode(recv2.at[h, kind], hq, k, side)
                total[hc * h + upper * hq + k] = value

    zq = cap // 4

    def z_copy(phase, d):
        src = zsend1.at[d - 1] if phase == 0 else zsend2
        dst = (zrecv1, zrecv2)[phase].at[d - 1]
        return remote(src, dst, z_send.at[phase, d - 1], z_recv.at[phase, d - 1], {"replica": (rep + d) % 4})

    for d in (2, 1, 3):
        for k in range(zq):
            encode(zsend1.at[d - 1], zq, k, total[(rep + d) % 4 * zq + k])
        go(z_copy(0, d))
    for d in (1, 2, 3):
        z_copy(0, d).wait_recv()
    for k in range(zq):
        value = total[rep * zq + k]
        for d in (1, 2, 3):
            value = value + decode(zrecv1.at[d - 1], zq, k, side)
        encode(zsend2, zq, k, value)
    for d in (2, 1, 3):
        go(z_copy(1, d))

    def put(buf, who):
        for k in range(zq):
            slot = who * zq + k
            value = decode(buf, zq, k, side)
            weight_grad[0, slot] = jnp.where(slot < shard_counts[0, shard], value, 0.0)

    put(zsend2, rep)
    for d in (1, 2, 3):
        z_copy(1, d).wait_recv()
        put(zrecv2.at[d - 1], (rep - d + 4) % 4)
    out_copy.wait()
    for copy in sent:
        copy.wait_send()


def body(inputs, kv_grad, weight_blocks, bitmap, counts):
    side = weight_blocks.shape[-1]
    cap = weight_blocks.shape[1]
    shards = counts.shape[1]
    slots = shards * cap
    tokens, width = inputs.shape
    cols = kv_grad.shape[1]
    places = bitmap.size
    groups = 8

    bits = bitmap.reshape(-1)
    ids = jnp.arange(places, dtype=jnp.int32)
    rank = jnp.sum(jnp.where(ids[None, :] < ids[:, None], bits[None, :], 0), axis=1)
    ends = jnp.cumsum(counts[0])
    passed = ends[None, :] <= rank[:, None]
    holder = jnp.sum(passed.astype(jnp.int32), axis=1)
    start = jnp.max(jnp.where(passed, ends[None, :], 0), axis=1)
    place_slot = jnp.where(bits == 1, holder * cap + rank - start, slots)
    slot_ids = jnp.arange(slots, dtype=jnp.int32)
    slot_place = jnp.sum(jnp.where(place_slot[None, :] == slot_ids[:, None], ids[None, :], 0), axis=1)

    n1, n2 = cap, cap // 4
    half = side // 2
    big, small = n1 * half + 8, n2 * half + 8
    anywhere = pl.BlockSpec(memory_space=pl.ANY)
    scalars = pl.BlockSpec(memory_space=pltpu.SMEM)
    return pl.pallas_call(
        kernel,
        out_shape=(
            jax.ShapeDtypeStruct(inputs.shape, jnp.bfloat16),
            jax.ShapeDtypeStruct(weight_blocks.shape, jnp.float32),
        ),
        in_specs=[scalars, scalars, scalars, anywhere, anywhere, anywhere],
        out_specs=(anywhere, pl.BlockSpec(memory_space=pltpu.VMEM)),
        scratch_shapes=[
            pltpu.VMEM((tokens, width), jnp.bfloat16),
            pltpu.VMEM((width, tokens), jnp.bfloat16),
            pltpu.VMEM((groups, tokens, cols), jnp.bfloat16),
            pltpu.VMEM((slots + 1, side, side), jnp.bfloat16),
            pltpu.VMEM((width, groups * cols), jnp.bfloat16),
            pltpu.VMEM((places, side, side), jnp.float32),
            pltpu.VMEM((tokens, width), jnp.bfloat16),
            pltpu.VMEM((2, 2 * cap, side, side), jnp.float32),
            pltpu.VMEM((cap, side, side), jnp.float32),
            pltpu.VMEM((2, 6, big, side), jnp.int32),
            pltpu.VMEM((2, 6, big, side), jnp.int32),
            pltpu.VMEM((2, 6, small, side), jnp.int32),
            pltpu.VMEM((2, 6, small, side), jnp.int32),
            pltpu.VMEM((3, small, side), jnp.int32),
            pltpu.VMEM((3, small, side), jnp.int32),
            pltpu.VMEM((small, side), jnp.int32),
            pltpu.VMEM((3, small, side), jnp.int32),
            pltpu.SemaphoreType.DMA((4,)),
            pltpu.SemaphoreType.DMA((7, PIECES)),
            pltpu.SemaphoreType.DMA((7, PIECES)),
            pltpu.SemaphoreType.DMA((2, 10, 2)),
            pltpu.SemaphoreType.DMA((2, 10, 2)),
            pltpu.SemaphoreType.DMA((2, 2, 6)),
            pltpu.SemaphoreType.DMA((2, 2, 6)),
            pltpu.SemaphoreType.DMA((2, 3)),
            pltpu.SemaphoreType.DMA((2, 3)),
        ],
        compiler_params=pltpu.CompilerParams(
            collective_id=0, has_side_effects=True, vmem_limit_bytes=48 * 1024 * 1024
        ),
    )(slot_place, place_slot, counts, inputs, kv_grad, weight_blocks)


def solution(mesh):
    in_specs = (
        P(("replica", "fsdp"), "tensor"),
        P(("replica", "fsdp"), "tensor"),
        P("tensor", "fsdp", None, None),
        P("tensor", None),
        P("tensor", None),
    )
    out_specs = (P(("replica", "fsdp"), "tensor"), P("tensor", "fsdp", None, None))
    return jax.shard_map(body, mesh=mesh, in_specs=in_specs, out_specs=out_specs, check_vma=False)
```

```python
import functools

import jax
import jax.numpy as jnp
from jax import lax
from jax.experimental import pallas as pl
from jax.experimental.pallas import tpu as pltpu
from jax.sharding import PartitionSpec as P

MESH = pl.DeviceIdType.MESH
RADIUS = 32700.0
STEPS = 16.0
LIFT = 2048.0
PIECES = 4
WAVES = ((0, 64), (64, 64))
M_R, M_L, O_R, O_L, C_R, C_L = range(6)


def encode(buf, count, k, block):
    half = block.shape[0] // 2
    peak = jnp.maximum(jnp.max(jnp.abs(block), axis=0, keepdims=True), 1e-30)
    code = (jnp.log(peak) * STEPS + LIFT).astype(jnp.int32) + 1
    scale = jnp.exp((code.astype(jnp.float32) - LIFT) * (1.0 / STEPS))
    whole = jnp.round(block * (RADIUS / scale)).astype(jnp.int32)
    buf[pl.ds(k * half, half), :] = whole[:half] * 65536 + whole[half:]
    buf[pl.ds(count * half + k, 1), :] = code


def decode(buf, count, k, height):
    half = height // 2
    pair = buf[pl.ds(k * half, half), :]
    code = buf[pl.ds(count * half + k, 1), :]
    scale = jnp.exp((code.astype(jnp.float32) - LIFT) * (1.0 / STEPS)) * (1.0 / RADIUS)
    low = (pair << 16) >> 16
    high = (pair - low) >> 16
    return jnp.concatenate([high.astype(jnp.float32), low.astype(jnp.float32)], axis=0) * scale


def number(bitmap, counts, cap):
    (height, width), shards = bitmap.shape, counts.shape[1]
    places = height * width

    def ids(shape, axis):
        return lax.broadcasted_iota(jnp.int32, shape, axis)

    spread = (ids((width, places), 1) % width == ids((width, places), 0)).astype(jnp.float32)
    wide = jnp.dot(bitmap.astype(jnp.float32), spread, preferred_element_type=jnp.float32)
    mine = ids((height, places), 1) // width == ids((height, places), 0)
    bits = jnp.sum(jnp.where(mine, wide, 0.0), axis=0, keepdims=True)
    before = (ids((places, places), 0) < ids((places, places), 1)).astype(jnp.float32)
    rank = jnp.dot(jnp.broadcast_to(bits, (height, places)), before, preferred_element_type=jnp.float32)[:1]
    square = (shards, shards)
    upto = ids(square, 1) <= ids(square, 0)
    ends = jnp.sum(jnp.where(upto, jnp.broadcast_to(counts, square).astype(jnp.float32), 0.0), axis=1, keepdims=True)
    passed = ends <= rank
    holder = jnp.sum(jnp.where(passed, 1.0, 0.0), axis=0, keepdims=True)
    start = jnp.max(jnp.where(passed, ends, 0.0), axis=0, keepdims=True)
    place_slot = jnp.where(bits > 0.5, holder * cap + rank - start, float(shards * cap))
    large = (places, places)
    down = jnp.sum(jnp.where(ids(large, 0) == ids(large, 1), place_slot, 0.0), axis=1, keepdims=True)
    held = down == ids(large, 1).astype(jnp.float32)
    slot_place = jnp.sum(jnp.where(held, ids(large, 0).astype(jnp.float32), 0.0), axis=0, keepdims=True)
    row = ids((8, places), 0)
    found = jnp.where(row == 0, slot_place, jnp.where(row == 1, place_slot, 0.0)).astype(jnp.int32)
    return jnp.clip(found, 0, jnp.where(row == 0, places - 1, shards * cap))


def kernel(
    shard_counts, inputs, kv_grad, weights, bitmap, counts,
    input_grad, weight_grad,
    bits_in, counts_in, tables, table, x_in, x_turned, kvg, wg, dense, terms, part, total,
    send1, recv1, send2, recv2, zsend1, zrecv1, zsend2, zrecv2,
    local_sem, kv_send, kv_recv, w_send, w_recv, rs_send, rs_recv, z_send, z_recv,
):
    rep = lax.axis_index("replica")
    shard = lax.axis_index("fsdp")
    band = lax.axis_index("tensor")
    tokens, width = x_in.shape
    side = terms.shape[-1]
    cap = weights.shape[1]
    cols = kv_grad.shape[1]
    hc = cap // 2
    ring = 4
    rows, groups = width // side, 8
    col_blocks = cols // side * groups
    piece = tokens // PIECES

    def shift(f, axis, by):
        y, x = f // ring, f % ring
        if axis == "x":
            return y * ring + (x + by + ring) % ring
        return ((y + by + ring) % ring) * ring + x

    def near(axis, by):
        return {"fsdp": shift(shard, axis, by)}

    def band_at(by):
        return (band + 2 * by + groups) % groups

    sibling = band + 1 - 2 * (band % 2)

    def sibling_at(by):
        return (sibling + 2 * by + groups) % groups

    def remote(src, dst, send_sem, recv_sem, where):
        return pltpu.make_async_remote_copy(
            src_ref=src, dst_ref=dst, send_sem=send_sem, recv_sem=recv_sem,
            device_id=where, device_id_type=MESH,
        )

    partners = [{"tensor": sibling}, {"tensor": band_at(1)}, {"tensor": band_at(-1)}]
    partners += [near(axis, by) for axis in ("x", "y") for by in (1, -1)]
    partners += [{"replica": (rep + d) % 4} for d in (1, 2, 3)]
    barrier = pltpu.get_barrier_semaphore()
    for where in partners:
        pl.semaphore_signal(barrier, inc=1, device_id=where, device_id_type=MESH)
    pl.semaphore_wait(barrier, len(partners))

    sent = []

    def go(copy):
        copy.start()
        sent.append(copy)

    def kv_at(b, p, n=1):
        return kvg.at[b, pl.ds(p * piece, n * piece), :]

    own_kv = [kv_grad.at[pl.ds(p * piece, piece), :] for p in range(PIECES)]
    right_order = list(range(PIECES))
    left_order = right_order[PIECES // 2:] + right_order[:PIECES // 2]
    for a, b in zip(right_order, left_order):
        go(remote(own_kv[a], kv_at(band, a), kv_send.at[0, a], kv_recv.at[0, a], {"tensor": band_at(1)}))
        go(remote(own_kv[b], kv_at(band, b), kv_send.at[1, b], kv_recv.at[1, b], {"tensor": band_at(-1)}))

    firsts = ("x", "y")
    seconds = ("y", "x")

    def w_at(f, slot, n):
        return wg.at[pl.ds(f * cap + slot, n)]

    for h in range(2):
        own_w = weights.at[0, pl.ds(hc * h, hc)]
        for d, by in ((0, 1), (1, -1)):
            go(remote(own_w, w_at(shard, hc * h, hc), w_send.at[h, 0, d], w_recv.at[h, 0, d], near(firsts[h], by)))
            go(remote(own_w, w_at(shard, hc * h, hc), w_send.at[h, 2, d], w_recv.at[h, 2, d], near(seconds[h], by)))
    go(remote(kv_grad, kv_at(band, 0, PIECES), kv_send.at[3, 0], kv_recv.at[3, 0], {"tensor": sibling}))
    local = [
        pltpu.make_async_copy(inputs, x_in, local_sem.at[0]),
        pltpu.make_async_copy(kv_grad, kvg.at[band], local_sem.at[1]),
        pltpu.make_async_copy(weights.at[0], w_at(shard, 0, cap), local_sem.at[2]),
        pltpu.make_async_copy(bitmap, bits_in, local_sem.at[3]),
        pltpu.make_async_copy(counts, counts_in, local_sem.at[4]),
    ]
    for copy in local:
        copy.start()

    def kv_wait(which, p, b, n=1):
        remote(kv_at(b, p, n), kv_at(b, p, n), kv_send.at[which, p], kv_recv.at[which, p], {"tensor": sibling}).wait_recv()

    def kv_pass(which, p, b):
        go(remote(kv_at(b, p), kv_at(b, p), kv_send.at[which, p], kv_recv.at[which, p], {"tensor": sibling}))

    def kv_relay(p, b, by):
        go(remote(kv_at(b, p), kv_at(b, p), kv_send.at[2, p], kv_recv.at[2, p], {"tensor": band_at(by)}))

    def w_wait(h, which, d, f, slot, n):
        at = w_at(f, hc * h + slot, n)
        remote(at, at, w_send.at[h, which, d], w_recv.at[h, which, d], {"tensor": sibling}).wait_recv()

    def w_go(h, which, d, f, slot, n, axis):
        at = w_at(f, hc * h + slot, n)
        go(remote(at, at, w_send.at[h, which, d], w_recv.at[h, which, d], near(axis, 1 if d == 0 else -1)))

    hq = hc // 2

    def w_first(h):
        for d, by in ((0, -1), (1, 1)):
            src = shift(shard, firsts[h], by)
            w_wait(h, 0, d, src, 0, hc)
            w_go(h, 1, d, src, d * hq, hq, firsts[h])
            for e in range(2):
                w_go(h, 3 + d, e, src, 0, hc, seconds[h])

    def w_far(h):
        src = shift(shard, firsts[h], 2)
        for d in range(2):
            w_wait(h, 1, d, src, d * hq, hq)
        for e in range(2):
            w_go(h, 5, e, src, 0, hc, seconds[h])

    def w_second(h, s):
        for d, by in ((0, -1), (1, 1)):
            src = shift(shift(shard, firsts[h], (0, -1, 1, 2)[s]), seconds[h], by)
            w_wait(h, 2 + s, d, src, 0, hc)
            w_go(h, 6 + s, d, src, d * hq, hq, seconds[h])

    def w_last(h, s):
        src = shift(shift(shard, firsts[h], (0, -1, 1, 2)[s]), seconds[h], 2)
        for d in range(2):
            w_wait(h, 6 + s, d, src, d * hq, hq)

    def outer(b):
        def tile(i, carry):
            at = pl.ds(pl.multiple_of(i * 2 * side, 2 * side), 2 * side)
            got = jnp.dot(x_turned[at, :], kvg[b], preferred_element_type=jnp.float32)
            for u in range(2):
                for v in range(2):
                    place = (2 * i + u) * col_blocks + 2 * b + v
                    terms[place] = got[u * side:(u + 1) * side, v * side:(v + 1) * side]
            return carry

        lax.fori_loop(0, rows // 2, tile, 0)

    local[3].wait()
    local[4].wait()
    tables[...] = number(bits_in[...], counts_in[...], cap)
    to_scalars = pltpu.make_async_copy(tables, table, local_sem.at[5])
    to_scalars.start()
    local[0].wait()
    local[1].wait()
    x_turned[...] = x_in[...].T
    for h in range(2):
        w_first(h)
    outer(band)
    to_scalars.wait()
    for p, q in ((0, 2), (1, 3)):
        kv_wait(0, p, band_at(-1))
        kv_relay(p, band_at(-1), 1)
        kv_wait(1, q, band_at(1))
        kv_relay(q, band_at(1), -1)
        kv_pass(4, p, band_at(-1))
        kv_pass(5, q, band_at(1))
        if p == 0:
            for h in range(2):
                w_far(h)
            for h in range(2):
                w_second(h, 0)
            kv_wait(3, 0, sibling, PIECES)
            outer(sibling)
    for s in range(1, 4):
        for h in range(2):
            w_second(h, s)
    for p, q in ((2, 0), (3, 1)):
        kv_wait(0, p, band_at(-1))
        kv_pass(4, p, band_at(-1))
        kv_wait(1, q, band_at(1))
        kv_pass(5, q, band_at(1))
    outer(band_at(-1))
    outer(band_at(1))
    for p in range(PIECES):
        kv_wait(4, p, sibling_at(-1))
        kv_wait(5, p, sibling_at(1))
    outer(sibling_at(-1))
    outer(sibling_at(1))
    for h in range(2):
        for s in range(4):
            w_last(h, s)
    local[2].wait()
    wg[wg.shape[0] - 1] = jnp.zeros((side, side), wg.dtype)

    def fill(i, carry):
        for j in range(col_blocks):
            place = i * col_blocks + j
            dense[pl.ds(pl.multiple_of(i * side, side), side), j * side:(j + 1) * side] = wg[jnp.clip(table[1, place], 0, wg.shape[0] - 1)]
        return carry

    lax.fori_loop(0, rows, fill, 0)
    for p in (0, 2, 1, 3):
        kv_wait(2, p, band_at(2))
        kv_pass(6, p, band_at(2))
    outer(band_at(2))
    for p in (0, 2, 1, 3):
        kv_wait(6, p, sibling_at(2))
    outer(sibling_at(2))

    n1 = ring * hq

    def coord(axis):
        return shard % ring if axis == "x" else shard // ring

    def owner(h, one, two):
        return two * ring + one if firsts[h] == "x" else one * ring + two

    def term1(w, h, one, k, upper):
        slot = owner(h, one, k // hq) * cap + hc * h + upper * hq + k % hq
        return terms[jnp.clip(table[0, slot], 0, terms.shape[0] - 1), pl.ds(WAVES[w][0], WAVES[w][1]), :]

    def tall(w, blocks):
        return pl.ds(0, blocks * WAVES[w][1] // 2 + 8)

    def own_part(w, h, two, upper, k):
        return part[w, h, two * hc + upper * hq + k, pl.ds(0, WAVES[w][1]), :]

    kinds = {M_R: (2, 0, 1), M_L: (2, 1, -1), O_R: (1, 1, 1), O_L: (-1, 0, -1), C_R: (1, 0, 1), C_L: (-1, 1, -1)}

    def rs_copy(phase, w, h, kind):
        axis = (firsts if phase == 0 else seconds)[h]
        src, dst = ((send1, recv1), (send2, recv2))[phase]
        blocks = (n1, hq)[phase]
        return remote(
            src.at[w, h, kind, tall(w, blocks)], dst.at[w, h, kind, tall(w, blocks)], rs_send.at[phase, w, h, kind], rs_recv.at[phase, w, h, kind],
            near(axis, kinds[kind][2]),
        )

    def first_send(w, pair):
        for kind in pair:
            for h in range(2):
                by, upper, _ = kinds[kind]
                one = (coord(firsts[h]) + by + ring) % ring
                relayed = {C_R: M_R, C_L: M_L}.get(kind)
                if relayed is not None:
                    rs_copy(0, w, h, relayed).wait_recv()

                for k in range(n1):
                    value = term1(w, h, one, k, upper)
                    if relayed is not None:
                        value = value + decode(recv1.at[w, h, relayed], n1, k, WAVES[w][1])
                    encode(send1.at[w, h, kind], n1, k, value)
                go(rs_copy(0, w, h, kind))

    def first_sum(w):
        for h in range(2):
            for kind in (O_R, O_L, C_R, C_L):
                rs_copy(0, w, h, kind).wait_recv()
            one = coord(firsts[h])

            for k in range(n1):
                for upper, pair in ((0, (C_R, O_L)), (1, (C_L, O_R))):
                    value = term1(w, h, one, k, upper)
                    for kind in pair:
                        value = value + decode(recv1.at[w, h, kind], n1, k, WAVES[w][1])
                    part[w, h, (k // hq) * hc + upper * hq + k % hq, pl.ds(0, WAVES[w][1]), :] = value

    def second_send(w, pair):
        relay = {C_R: M_R, C_L: M_L}
        both = [(kind, h) for kind in pair for h in range(2)]
        for kind, h in both:
            if kind in relay:
                rs_copy(1, w, h, relay[kind]).wait_recv()
        for kind, h in both:
            by, upper, _ = kinds[kind]
            two = (coord(seconds[h]) + by + ring) % ring
            for k in range(hq):
                value = own_part(w, h, two, upper, k)
                if kind in relay:
                    value = value + decode(recv2.at[w, h, relay[kind]], hq, k, WAVES[w][1])
                encode(send2.at[w, h, kind], hq, k, value)
        for kind, h in both:
            go(rs_copy(1, w, h, kind))

    def second_sum(w):
        for h in range(2):
            for kind in (O_R, O_L, C_R, C_L):
                rs_copy(1, w, h, kind).wait_recv()
        for h in range(2):
            two = coord(seconds[h])
            for upper, pair in ((0, (C_R, O_L)), (1, (C_L, O_R))):
                for k in range(hq):
                    value = own_part(w, h, two, upper, k)
                    for kind in pair:
                        value = value + decode(recv2.at[w, h, kind], hq, k, WAVES[w][1])
                    total[hc * h + upper * hq + k, pl.ds(WAVES[w][0], WAVES[w][1]), :] = value

    zq = cap // 4

    def z_copy(phase, w, d):
        src = zsend1.at[w, d - 1, tall(w, zq)] if phase == 0 else zsend2.at[w, tall(w, zq)]
        dst = (zrecv1, zrecv2)[phase].at[w, d - 1, tall(w, zq)]
        return remote(src, dst, z_send.at[phase, w, d - 1], z_recv.at[phase, w, d - 1], {"replica": (rep + d) % 4})

    def summed(w, who, k):
        return total[who * zq + k, pl.ds(WAVES[w][0], WAVES[w][1]), :]

    def z_scatter(w):
        for d in (2, 1, 3):
            for k in range(zq):
                encode(zsend1.at[w, d - 1], zq, k, summed(w, (rep + d) % 4, k))
        for d in (2, 1, 3):
            go(z_copy(0, w, d))

    def put(buf, w, who):
        for k in range(zq):
            slot = who * zq + k
            value = decode(buf, zq, k, WAVES[w][1])
            weight_grad[0, slot, pl.ds(WAVES[w][0], WAVES[w][1]), :] = jnp.where(slot < shard_counts[0, shard], value, 0.0)

    def z_hand(w):
        for d in (1, 3, 2):
            z_copy(0, w, d).wait_recv()
        for k in range(zq):
            value = summed(w, rep, k)
            for d in (1, 3, 2):
                value = value + decode(zrecv1.at[w, d - 1], zq, k, WAVES[w][1])
            encode(zsend2.at[w], zq, k, value)
        for d in (2, 1, 3):
            go(z_copy(1, w, d))
        put(zsend2.at[w], w, rep)

    def z_take(w):
        for d in (1, 3, 2):
            z_copy(1, w, d).wait_recv()
        for d in (1, 3, 2):
            put(zrecv2.at[w, d - 1], w, (rep - d + 4) % 4)

    def product(i, carry):
        at = pl.ds(pl.multiple_of(i * 2 * side, 2 * side), 2 * side)
        acc = jnp.zeros((tokens, 2 * side), jnp.float32)
        for b in range(groups):
            acc = acc + lax.dot_general(
                kvg[b], dense[at, b * cols:(b + 1) * cols], (((1,), (1,)), ((), ())),
                preferred_element_type=jnp.float32,
            )
        input_grad[:, at] = acc.astype(input_grad.dtype)
        return carry

    early, alone, late = (M_R, M_L), (O_R, O_L), (C_R, C_L)
    first_send(0, early)
    first_send(0, alone)
    first_send(0, late)
    first_send(1, early)
    first_send(1, alone)
    first_sum(0)
    second_send(0, early)
    second_send(0, alone)
    first_send(1, late)
    second_send(0, late)
    first_sum(1)
    second_send(1, early)
    second_send(1, alone)
    second_sum(0)
    z_scatter(0)
    second_send(1, late)
    z_hand(0)
    second_sum(1)
    z_scatter(1)
    lax.fori_loop(0, rows // 2, product, 0)
    z_take(0)
    z_hand(1)
    z_take(1)
    for copy in sent:
        copy.wait_send()


def body(inputs, kv_grad, weight_blocks, bitmap, counts):
    side = weight_blocks.shape[-1]
    cap = weight_blocks.shape[1]
    shards = counts.shape[1]
    slots = shards * cap
    tokens, width = inputs.shape
    cols = kv_grad.shape[1]
    places = bitmap.size
    groups = 8
    waves, half = len(WAVES), max(n for _, n in WAVES) // 2
    big, small = cap * half + 8, cap // 4 * half + 8
    held = pl.BlockSpec(memory_space=pltpu.HBM)
    fast = pl.BlockSpec(memory_space=pltpu.VMEM)
    scalars = pl.BlockSpec(memory_space=pltpu.SMEM)
    return pl.pallas_call(
        kernel,
        out_shape=(
            jax.ShapeDtypeStruct(inputs.shape, jnp.bfloat16),
            jax.ShapeDtypeStruct(weight_blocks.shape, jnp.float32),
        ),
        in_specs=[scalars, held, held, held, held, held],
        out_specs=(fast, fast),
        scratch_shapes=[
            pltpu.VMEM(bitmap.shape, jnp.int32),
            pltpu.VMEM(counts.shape, jnp.int32),
            pltpu.VMEM((8, places), jnp.int32),
            pltpu.SMEM((8, places), jnp.int32),
            pltpu.VMEM((tokens, width), jnp.bfloat16),
            pltpu.VMEM((width, tokens), jnp.bfloat16),
            pltpu.VMEM((groups, tokens, cols), jnp.bfloat16),
            pltpu.VMEM((slots + 1, side, side), jnp.bfloat16),
            pltpu.VMEM((width, groups * cols), jnp.bfloat16),
            pltpu.VMEM((places, side, side), jnp.float32),
            pltpu.VMEM((waves, 2, 2 * cap, 2 * half, side), jnp.float32),
            pltpu.VMEM((cap, side, side), jnp.float32),
            pltpu.VMEM((waves, 2, 6, big, side), jnp.int32),
            pltpu.VMEM((waves, 2, 6, big, side), jnp.int32),
            pltpu.VMEM((waves, 2, 6, small, side), jnp.int32),
            pltpu.VMEM((waves, 2, 6, small, side), jnp.int32),
            pltpu.VMEM((waves, 3, small, side), jnp.int32),
            pltpu.VMEM((waves, 3, small, side), jnp.int32),
            pltpu.VMEM((waves, small, side), jnp.int32),
            pltpu.VMEM((waves, 3, small, side), jnp.int32),
            pltpu.SemaphoreType.DMA((6,)),
            pltpu.SemaphoreType.DMA((7, PIECES)),
            pltpu.SemaphoreType.DMA((7, PIECES)),
            pltpu.SemaphoreType.DMA((2, 10, 2)),
            pltpu.SemaphoreType.DMA((2, 10, 2)),
            pltpu.SemaphoreType.DMA((2, waves, 2, 6)),
            pltpu.SemaphoreType.DMA((2, waves, 2, 6)),
            pltpu.SemaphoreType.DMA((2, waves, 3)),
            pltpu.SemaphoreType.DMA((2, waves, 3)),
        ],
        compiler_params=pltpu.CompilerParams(
            collective_id=0, has_side_effects=True, vmem_limit_bytes=48 * 1024 * 1024
        ),
    )(counts, *(pltpu.with_memory_space_constraint(a, pltpu.HBM) for a in (inputs, kv_grad, weight_blocks, bitmap, counts)))


def solution(mesh):
    in_specs = (
        P(("replica", "fsdp"), "tensor"),
        P(("replica", "fsdp"), "tensor"),
        P("tensor", "fsdp", None, None),
        P("tensor", None),
        P("tensor", None),
    )
    out_specs = (P(("replica", "fsdp"), "tensor"), P("tensor", "fsdp", None, None))
    return jax.shard_map(body, mesh=mesh, in_specs=in_specs, out_specs=out_specs, check_vma=False)
```

```python
import functools

import jax
import jax.numpy as jnp
from jax import lax
from jax.experimental import pallas as pl
from jax.experimental.pallas import tpu as pltpu
from jax.sharding import PartitionSpec as P

MESH = pl.DeviceIdType.MESH
RADIUS = 32700.0
STEPS = 16.0
LIFT = 2048.0
PIECES = 4
WAVES = ((0, 64), (64, 64))
M_R, M_L, O_R, O_L, C_R, C_L = range(6)


def encode(buf, count, k, block):
    half = block.shape[0] // 2
    peak = jnp.maximum(jnp.max(jnp.abs(block), axis=0, keepdims=True), 1e-30)
    code = (jnp.log(peak) * STEPS + LIFT).astype(jnp.int32) + 1
    scale = jnp.exp((code.astype(jnp.float32) - LIFT) * (1.0 / STEPS))
    whole = jnp.round(block * (RADIUS / scale)).astype(jnp.int32)
    buf[pl.ds(k * half, half), :] = whole[:half] * 65536 + whole[half:]
    buf[pl.ds(count * half + k, 1), :] = code


def decode(buf, count, k, height):
    half = height // 2
    pair = buf[pl.ds(k * half, half), :]
    code = buf[pl.ds(count * half + k, 1), :]
    scale = jnp.exp((code.astype(jnp.float32) - LIFT) * (1.0 / STEPS)) * (1.0 / RADIUS)
    low = (pair << 16) >> 16
    high = (pair - low) >> 16
    return jnp.concatenate([high.astype(jnp.float32), low.astype(jnp.float32)], axis=0) * scale


def number(bitmap, counts, cap):
    (height, width), shards = bitmap.shape, counts.shape[1]
    places = height * width

    def ids(shape, axis):
        return lax.broadcasted_iota(jnp.int32, shape, axis)

    spread = (ids((width, places), 1) % width == ids((width, places), 0)).astype(jnp.float32)
    wide = jnp.dot(bitmap.astype(jnp.float32), spread, preferred_element_type=jnp.float32)
    mine = ids((height, places), 1) // width == ids((height, places), 0)
    bits = jnp.sum(jnp.where(mine, wide, 0.0), axis=0, keepdims=True)
    before = (ids((places, places), 0) < ids((places, places), 1)).astype(jnp.float32)
    rank = jnp.dot(jnp.broadcast_to(bits, (height, places)), before, preferred_element_type=jnp.float32)[:1]
    square = (shards, shards)
    upto = ids(square, 1) <= ids(square, 0)
    ends = jnp.sum(jnp.where(upto, jnp.broadcast_to(counts, square).astype(jnp.float32), 0.0), axis=1, keepdims=True)
    passed = ends <= rank
    holder = jnp.sum(jnp.where(passed, 1.0, 0.0), axis=0, keepdims=True)
    start = jnp.max(jnp.where(passed, ends, 0.0), axis=0, keepdims=True)
    place_slot = jnp.where(bits > 0.5, holder * cap + rank - start, float(shards * cap))
    large = (places, places)
    down = jnp.sum(jnp.where(ids(large, 0) == ids(large, 1), place_slot, 0.0), axis=1, keepdims=True)
    held = down == ids(large, 1).astype(jnp.float32)
    slot_place = jnp.sum(jnp.where(held, ids(large, 0).astype(jnp.float32), 0.0), axis=0, keepdims=True)
    row = ids((8, places), 0)
    found = jnp.where(row == 0, slot_place, jnp.where(row == 1, place_slot, 0.0)).astype(jnp.int32)
    return jnp.clip(found, 0, jnp.where(row == 0, places - 1, shards * cap))


def kernel(
    shard_counts, inputs, kv_grad, weights, bitmap, counts,
    input_grad, weight_grad,
    bits_in, counts_in, tables, table, x_in, x_turned, kvg, wg, dense, terms, part, total,
    send1, recv1, send2, recv2, zsend1, zrecv1, zsend2, zrecv2,
    local_sem, kv_send, kv_recv, w_send, w_recv, rs_send, rs_recv, z_send, z_recv,
):
    rep = lax.axis_index("replica")
    shard = lax.axis_index("fsdp")
    band = lax.axis_index("tensor")
    tokens, width = x_in.shape
    side = terms.shape[-1]
    cap = weights.shape[1]
    cols = kv_grad.shape[1]
    hc = cap // 2
    ring = 4
    rows, groups = width // side, 8
    col_blocks = cols // side * groups
    piece = tokens // PIECES

    def shift(f, axis, by):
        y, x = f // ring, f % ring
        if axis == "x":
            return y * ring + (x + by + ring) % ring
        return ((y + by + ring) % ring) * ring + x

    def near(axis, by):
        return {"fsdp": shift(shard, axis, by)}

    def band_at(by):
        return (band + 2 * by + groups) % groups

    sibling = band + 1 - 2 * (band % 2)

    def sibling_at(by):
        return (sibling + 2 * by + groups) % groups

    def remote(src, dst, send_sem, recv_sem, where):
        return pltpu.make_async_remote_copy(
            src_ref=src, dst_ref=dst, send_sem=send_sem, recv_sem=recv_sem,
            device_id=where, device_id_type=MESH,
        )

    partners = [{"tensor": sibling}, {"tensor": band_at(1)}, {"tensor": band_at(-1)}]
    partners += [near(axis, by) for axis in ("x", "y") for by in (1, -1, 2)]
    partners += [{"replica": (rep + d) % 4} for d in (1, 2, 3)]
    barrier = pltpu.get_barrier_semaphore()
    for where in partners:
        pl.semaphore_signal(barrier, inc=1, device_id=where, device_id_type=MESH)
    pl.semaphore_wait(barrier, len(partners))

    sent = []

    def go(copy):
        copy.start()
        sent.append(copy)

    def kv_at(b, p, n=1):
        return kvg.at[b, pl.ds(p * piece, n * piece), :]

    own_kv = [kv_grad.at[pl.ds(p * piece, piece), :] for p in range(PIECES)]
    right_order = list(range(PIECES))
    left_order = right_order[PIECES // 2:] + right_order[:PIECES // 2]
    for a, b in zip(right_order, left_order):
        go(remote(own_kv[a], kv_at(band, a), kv_send.at[0, a], kv_recv.at[0, a], {"tensor": band_at(1)}))
        go(remote(own_kv[b], kv_at(band, b), kv_send.at[1, b], kv_recv.at[1, b], {"tensor": band_at(-1)}))

    firsts = ("x", "y")
    seconds = ("y", "x")

    def w_at(f, slot, n):
        return wg.at[pl.ds(f * cap + slot, n)]

    for h in range(2):
        own_w = weights.at[0, pl.ds(hc * h, hc)]
        for d, by in ((0, 1), (1, -1)):
            go(remote(own_w, w_at(shard, hc * h, hc), w_send.at[h, 0, d], w_recv.at[h, 0, d], near(firsts[h], by)))
            go(remote(own_w, w_at(shard, hc * h, hc), w_send.at[h, 2, d], w_recv.at[h, 2, d], near(seconds[h], by)))
    go(remote(kv_grad, kv_at(band, 0, PIECES), kv_send.at[3, 0], kv_recv.at[3, 0], {"tensor": sibling}))
    local = [
        pltpu.make_async_copy(inputs, x_in, local_sem.at[0]),
        pltpu.make_async_copy(kv_grad, kvg.at[band], local_sem.at[1]),
        pltpu.make_async_copy(weights.at[0], w_at(shard, 0, cap), local_sem.at[2]),
        pltpu.make_async_copy(bitmap, bits_in, local_sem.at[3]),
        pltpu.make_async_copy(counts, counts_in, local_sem.at[4]),
    ]
    for copy in local:
        copy.start()

    def kv_wait(which, p, b, n=1):
        remote(kv_at(b, p, n), kv_at(b, p, n), kv_send.at[which, p], kv_recv.at[which, p], {"tensor": sibling}).wait_recv()

    def kv_pass(which, p, b):
        go(remote(kv_at(b, p), kv_at(b, p), kv_send.at[which, p], kv_recv.at[which, p], {"tensor": sibling}))

    def kv_relay(p, b, by):
        go(remote(kv_at(b, p), kv_at(b, p), kv_send.at[2, p], kv_recv.at[2, p], {"tensor": band_at(by)}))

    def w_wait(h, which, d, f, slot, n):
        at = w_at(f, hc * h + slot, n)
        remote(at, at, w_send.at[h, which, d], w_recv.at[h, which, d], {"tensor": sibling}).wait_recv()

    def w_go(h, which, d, f, slot, n, axis):
        at = w_at(f, hc * h + slot, n)
        go(remote(at, at, w_send.at[h, which, d], w_recv.at[h, which, d], near(axis, 1 if d == 0 else -1)))

    hq = hc // 2

    def w_first(h):
        for d, by in ((0, -1), (1, 1)):
            src = shift(shard, firsts[h], by)
            w_wait(h, 0, d, src, 0, hc)
            w_go(h, 1, d, src, d * hq, hq, firsts[h])
            for e in range(2):
                w_go(h, 3 + d, e, src, 0, hc, seconds[h])

    def w_far(h):
        src = shift(shard, firsts[h], 2)
        for d in range(2):
            w_wait(h, 1, d, src, d * hq, hq)
        for e in range(2):
            w_go(h, 5, e, src, 0, hc, seconds[h])

    def w_second(h, s):
        for d, by in ((0, -1), (1, 1)):
            src = shift(shift(shard, firsts[h], (0, -1, 1, 2)[s]), seconds[h], by)
            w_wait(h, 2 + s, d, src, 0, hc)
            w_go(h, 6 + s, d, src, d * hq, hq, seconds[h])

    def w_last(h, s):
        src = shift(shift(shard, firsts[h], (0, -1, 1, 2)[s]), seconds[h], 2)
        for d in range(2):
            w_wait(h, 6 + s, d, src, d * hq, hq)

    def outer(b):
        def tile(i, carry):
            at = pl.ds(pl.multiple_of(i * 2 * side, 2 * side), 2 * side)
            got = jnp.dot(x_turned[at, :], kvg[b], preferred_element_type=jnp.float32)
            for u in range(2):
                for v in range(2):
                    place = (2 * i + u) * col_blocks + 2 * b + v
                    terms[place] = got[u * side:(u + 1) * side, v * side:(v + 1) * side]
            return carry

        lax.fori_loop(0, rows // 2, tile, 0)

    local[3].wait()
    local[4].wait()
    tables[...] = number(bits_in[...], counts_in[...], cap)
    to_scalars = pltpu.make_async_copy(tables, table, local_sem.at[5])
    to_scalars.start()
    local[0].wait()
    local[1].wait()
    x_turned[...] = x_in[...].T
    for h in range(2):
        w_first(h)
    outer(band)
    to_scalars.wait()
    for p, q in ((0, 2), (1, 3)):
        kv_wait(0, p, band_at(-1))
        kv_relay(p, band_at(-1), 1)
        kv_wait(1, q, band_at(1))
        kv_relay(q, band_at(1), -1)
        kv_pass(4, p, band_at(-1))
        kv_pass(5, q, band_at(1))
        if p == 0:
            for h in range(2):
                w_far(h)
            for h in range(2):
                w_second(h, 0)
            kv_wait(3, 0, sibling, PIECES)
            outer(sibling)
    for s in range(1, 4):
        for h in range(2):
            w_second(h, s)
    for p, q in ((2, 0), (3, 1)):
        kv_wait(0, p, band_at(-1))
        kv_pass(4, p, band_at(-1))
        kv_wait(1, q, band_at(1))
        kv_pass(5, q, band_at(1))
    outer(band_at(-1))
    outer(band_at(1))
    for p in range(PIECES):
        kv_wait(4, p, sibling_at(-1))
        kv_wait(5, p, sibling_at(1))
    outer(sibling_at(-1))
    outer(sibling_at(1))
    for h in range(2):
        for s in range(4):
            w_last(h, s)
    local[2].wait()
    wg[wg.shape[0] - 1] = jnp.zeros((side, side), wg.dtype)

    def fill(i, carry):
        for j in range(col_blocks):
            place = i * col_blocks + j
            dense[pl.ds(pl.multiple_of(i * side, side), side), j * side:(j + 1) * side] = wg[jnp.clip(table[1, place], 0, wg.shape[0] - 1)]
        return carry

    lax.fori_loop(0, rows, fill, 0)
    for p in (0, 2, 1, 3):
        kv_wait(2, p, band_at(2))
        kv_pass(6, p, band_at(2))
    outer(band_at(2))
    for p in (0, 2, 1, 3):
        kv_wait(6, p, sibling_at(2))
    outer(sibling_at(2))

    n1 = ring * hq

    def coord(axis):
        return shard % ring if axis == "x" else shard // ring

    def owner(h, one, two):
        return two * ring + one if firsts[h] == "x" else one * ring + two

    def term1(w, h, one, k, upper):
        slot = owner(h, one, k // hq) * cap + hc * h + upper * hq + k % hq
        return terms[jnp.clip(table[0, slot], 0, terms.shape[0] - 1), pl.ds(WAVES[w][0], WAVES[w][1]), :]

    def tall(w, blocks):
        return pl.ds(0, blocks * WAVES[w][1] // 2 + 8)

    def own_part(w, h, two, upper, k):
        return part[w, h, two * hc + upper * hq + k, pl.ds(0, WAVES[w][1]), :]

    kinds = {M_R: (2, 0, 1), M_L: (2, 1, -1), O_R: (1, 1, 1), O_L: (-1, 0, -1), C_R: (1, 0, 1), C_L: (-1, 1, -1)}

    def rs_copy(phase, w, h, kind):
        axis = (firsts if phase == 0 else seconds)[h]
        src, dst = ((send1, recv1), (send2, recv2))[phase]
        blocks = (n1, hq)[phase]
        return remote(
            src.at[w, h, kind, tall(w, blocks)], dst.at[w, h, kind, tall(w, blocks)], rs_send.at[phase, w, h, kind], rs_recv.at[phase, w, h, kind],
            near(axis, kinds[kind][0] if phase == 1 else kinds[kind][2]),
        )

    def first_send(w, pair):
        for kind in pair:
            for h in range(2):
                by, upper, _ = kinds[kind]
                one = (coord(firsts[h]) + by + ring) % ring
                relayed = {C_R: M_R, C_L: M_L}.get(kind)
                if relayed is not None:
                    rs_copy(0, w, h, relayed).wait_recv()

                for k in range(n1):
                    value = term1(w, h, one, k, upper)
                    if relayed is not None:
                        value = value + decode(recv1.at[w, h, relayed], n1, k, WAVES[w][1])
                    encode(send1.at[w, h, kind], n1, k, value)
                go(rs_copy(0, w, h, kind))

    def first_sum(w):
        for h in range(2):
            for kind in (O_R, O_L, C_R, C_L):
                rs_copy(0, w, h, kind).wait_recv()
            one = coord(firsts[h])

            for k in range(n1):
                for upper, pair in ((0, (C_R, O_L)), (1, (C_L, O_R))):
                    value = term1(w, h, one, k, upper)
                    for kind in pair:
                        value = value + decode(recv1.at[w, h, kind], n1, k, WAVES[w][1])
                    part[w, h, (k // hq) * hc + upper * hq + k % hq, pl.ds(0, WAVES[w][1]), :] = value

    def second_send(w):
        for h in range(2):
            for kind in range(6):
                by, upper, _ = kinds[kind]
                two = (coord(seconds[h]) + by + ring) % ring
                for k in range(hq):
                    encode(send2.at[w, h, kind], hq, k, own_part(w, h, two, upper, k))
            for kind in range(6):
                go(rs_copy(1, w, h, kind))

    def second_sum(w):
        for h in range(2):
            for kind in range(6):
                rs_copy(1, w, h, kind).wait_recv()
        for h in range(2):
            two = coord(seconds[h])
            for upper, three in ((0, (C_R, O_L, M_R)), (1, (C_L, O_R, M_L))):
                for k in range(hq):
                    value = own_part(w, h, two, upper, k)
                    for kind in three:
                        value = value + decode(recv2.at[w, h, kind], hq, k, WAVES[w][1])
                    total[hc * h + upper * hq + k, pl.ds(WAVES[w][0], WAVES[w][1]), :] = value

    zq = cap // 4

    def z_copy(phase, w, d):
        src = zsend1.at[w, d - 1, tall(w, zq)] if phase == 0 else zsend2.at[w, tall(w, zq)]
        dst = (zrecv1, zrecv2)[phase].at[w, d - 1, tall(w, zq)]
        return remote(src, dst, z_send.at[phase, w, d - 1], z_recv.at[phase, w, d - 1], {"replica": (rep + d) % 4})

    def summed(w, who, k):
        return total[who * zq + k, pl.ds(WAVES[w][0], WAVES[w][1]), :]

    def z_scatter(w):
        for d in (2, 1, 3):
            for k in range(zq):
                encode(zsend1.at[w, d - 1], zq, k, summed(w, (rep + d) % 4, k))
        for d in (2, 1, 3):
            go(z_copy(0, w, d))

    def put(buf, w, who):
        for k in range(zq):
            slot = who * zq + k
            value = decode(buf, zq, k, WAVES[w][1])
            weight_grad[0, slot, pl.ds(WAVES[w][0], WAVES[w][1]), :] = jnp.where(slot < shard_counts[0, shard], value, 0.0)

    def z_hand(w):
        for d in (1, 3, 2):
            z_copy(0, w, d).wait_recv()
        for k in range(zq):
            value = summed(w, rep, k)
            for d in (1, 3, 2):
                value = value + decode(zrecv1.at[w, d - 1], zq, k, WAVES[w][1])
            encode(zsend2.at[w], zq, k, value)
        for d in (2, 1, 3):
            go(z_copy(1, w, d))
        put(zsend2.at[w], w, rep)

    def z_take(w):
        for d in (1, 3, 2):
            z_copy(1, w, d).wait_recv()
        for d in (1, 3, 2):
            put(zrecv2.at[w, d - 1], w, (rep - d + 4) % 4)

    def product(i, carry):
        at = pl.ds(pl.multiple_of(i * 2 * side, 2 * side), 2 * side)
        acc = jnp.zeros((tokens, 2 * side), jnp.float32)
        for b in range(groups):
            acc = acc + lax.dot_general(
                kvg[b], dense[at, b * cols:(b + 1) * cols], (((1,), (1,)), ((), ())),
                preferred_element_type=jnp.float32,
            )
        input_grad[:, at] = acc.astype(input_grad.dtype)
        return carry

    early, alone, late = (M_R, M_L), (O_R, O_L), (C_R, C_L)
    first_send(0, early)
    first_send(0, alone)
    first_send(0, late)
    first_send(1, early)
    first_send(1, alone)
    lax.fori_loop(0, rows // 2, product, 0)
    first_sum(0)
    second_send(0)
    first_send(1, late)
    second_sum(0)
    z_scatter(0)
    first_sum(1)
    second_send(1)
    z_hand(0)
    second_sum(1)
    z_scatter(1)
    z_take(0)
    z_hand(1)
    z_take(1)
    for copy in sent:
        copy.wait_send()


def body(inputs, kv_grad, weight_blocks, bitmap, counts):
    side = weight_blocks.shape[-1]
    cap = weight_blocks.shape[1]
    shards = counts.shape[1]
    slots = shards * cap
    tokens, width = inputs.shape
    cols = kv_grad.shape[1]
    places = bitmap.size
    groups = 8
    waves, half = len(WAVES), max(n for _, n in WAVES) // 2
    big, small = cap * half + 8, cap // 4 * half + 8
    held = pl.BlockSpec(memory_space=pltpu.HBM)
    fast = pl.BlockSpec(memory_space=pltpu.VMEM)
    scalars = pl.BlockSpec(memory_space=pltpu.SMEM)
    return pl.pallas_call(
        kernel,
        out_shape=(
            jax.ShapeDtypeStruct(inputs.shape, jnp.bfloat16),
            jax.ShapeDtypeStruct(weight_blocks.shape, jnp.float32),
        ),
        in_specs=[scalars, held, held, held, held, held],
        out_specs=(fast, fast),
        scratch_shapes=[
            pltpu.VMEM(bitmap.shape, jnp.int32),
            pltpu.VMEM(counts.shape, jnp.int32),
            pltpu.VMEM((8, places), jnp.int32),
            pltpu.SMEM((8, places), jnp.int32),
            pltpu.VMEM((tokens, width), jnp.bfloat16),
            pltpu.VMEM((width, tokens), jnp.bfloat16),
            pltpu.VMEM((groups, tokens, cols), jnp.bfloat16),
            pltpu.VMEM((slots + 1, side, side), jnp.bfloat16),
            pltpu.VMEM((width, groups * cols), jnp.bfloat16),
            pltpu.VMEM((places, side, side), jnp.float32),
            pltpu.VMEM((waves, 2, 2 * cap, 2 * half, side), jnp.float32),
            pltpu.VMEM((cap, side, side), jnp.float32),
            pltpu.VMEM((waves, 2, 6, big, side), jnp.int32),
            pltpu.VMEM((waves, 2, 6, big, side), jnp.int32),
            pltpu.VMEM((waves, 2, 6, small, side), jnp.int32),
            pltpu.VMEM((waves, 2, 6, small, side), jnp.int32),
            pltpu.VMEM((waves, 3, small, side), jnp.int32),
            pltpu.VMEM((waves, 3, small, side), jnp.int32),
            pltpu.VMEM((waves, small, side), jnp.int32),
            pltpu.VMEM((waves, 3, small, side), jnp.int32),
            pltpu.SemaphoreType.DMA((6,)),
            pltpu.SemaphoreType.DMA((7, PIECES)),
            pltpu.SemaphoreType.DMA((7, PIECES)),
            pltpu.SemaphoreType.DMA((2, 10, 2)),
            pltpu.SemaphoreType.DMA((2, 10, 2)),
            pltpu.SemaphoreType.DMA((2, waves, 2, 6)),
            pltpu.SemaphoreType.DMA((2, waves, 2, 6)),
            pltpu.SemaphoreType.DMA((2, waves, 3)),
            pltpu.SemaphoreType.DMA((2, waves, 3)),
        ],
        compiler_params=pltpu.CompilerParams(
            collective_id=0, has_side_effects=True, vmem_limit_bytes=48 * 1024 * 1024
        ),
    )(counts, *(pltpu.with_memory_space_constraint(a, pltpu.HBM) for a in (inputs, kv_grad, weight_blocks, bitmap, counts)))


def solution(mesh):
    in_specs = (
        P(("replica", "fsdp"), "tensor"),
        P(("replica", "fsdp"), "tensor"),
        P("tensor", "fsdp", None, None),
        P("tensor", None),
        P("tensor", None),
    )
    out_specs = (P(("replica", "fsdp"), "tensor"), P("tensor", "fsdp", None, None))
    return jax.shard_map(body, mesh=mesh, in_specs=in_specs, out_specs=out_specs, check_vma=False)
```

```python
import functools

import jax
import jax.numpy as jnp
from jax import lax
from jax.experimental import pallas as pl
from jax.experimental.pallas import tpu as pltpu
from jax.sharding import PartitionSpec as P

MESH = pl.DeviceIdType.MESH
RADIUS = 32700.0
STEPS = 16.0
LIFT = 2048.0
PIECES = 4
WAVES = ((0, 64), (64, 64))
M_R, M_L, O_R, O_L, C_R, C_L = range(6)


def encode(buf, count, k, block):
    half = block.shape[0] // 2
    peak = jnp.maximum(jnp.max(jnp.abs(block), axis=0, keepdims=True), 1e-30)
    code = (jnp.log(peak) * STEPS + LIFT).astype(jnp.int32) + 1
    scale = jnp.exp((code.astype(jnp.float32) - LIFT) * (1.0 / STEPS))
    whole = jnp.round(block * (RADIUS / scale)).astype(jnp.int32)
    buf[pl.ds(k * half, half), :] = whole[:half] * 65536 + whole[half:]
    buf[pl.ds(count * half + k, 1), :] = code


def decode(buf, count, k, height):
    half = height // 2
    pair = buf[pl.ds(k * half, half), :]
    code = buf[pl.ds(count * half + k, 1), :]
    scale = jnp.exp((code.astype(jnp.float32) - LIFT) * (1.0 / STEPS)) * (1.0 / RADIUS)
    low = (pair << 16) >> 16
    high = (pair - low) >> 16
    return jnp.concatenate([high.astype(jnp.float32), low.astype(jnp.float32)], axis=0) * scale


def number(bitmap, counts, cap):
    (height, width), shards = bitmap.shape, counts.shape[1]
    places = height * width

    def ids(shape, axis):
        return lax.broadcasted_iota(jnp.int32, shape, axis)

    spread = (ids((width, places), 1) % width == ids((width, places), 0)).astype(jnp.float32)
    wide = jnp.dot(bitmap.astype(jnp.float32), spread, preferred_element_type=jnp.float32)
    mine = ids((height, places), 1) // width == ids((height, places), 0)
    bits = jnp.sum(jnp.where(mine, wide, 0.0), axis=0, keepdims=True)
    before = (ids((places, places), 0) < ids((places, places), 1)).astype(jnp.float32)
    rank = jnp.dot(jnp.broadcast_to(bits, (height, places)), before, preferred_element_type=jnp.float32)[:1]
    square = (shards, shards)
    upto = ids(square, 1) <= ids(square, 0)
    ends = jnp.sum(jnp.where(upto, jnp.broadcast_to(counts, square).astype(jnp.float32), 0.0), axis=1, keepdims=True)
    passed = ends <= rank
    holder = jnp.sum(jnp.where(passed, 1.0, 0.0), axis=0, keepdims=True)
    start = jnp.max(jnp.where(passed, ends, 0.0), axis=0, keepdims=True)
    place_slot = jnp.where(bits > 0.5, holder * cap + rank - start, float(shards * cap))
    large = (places, places)
    down = jnp.sum(jnp.where(ids(large, 0) == ids(large, 1), place_slot, 0.0), axis=1, keepdims=True)
    held = down == ids(large, 1).astype(jnp.float32)
    slot_place = jnp.sum(jnp.where(held, ids(large, 0).astype(jnp.float32), 0.0), axis=0, keepdims=True)
    row = ids((8, places), 0)
    found = jnp.where(row == 0, slot_place, jnp.where(row == 1, place_slot, 0.0)).astype(jnp.int32)
    return jnp.clip(found, 0, jnp.where(row == 0, places - 1, shards * cap))


def kernel(
    shard_counts, inputs, kv_grad, weights, bitmap, counts,
    input_grad, weight_grad,
    bits_in, counts_in, tables, table, x_in, x_turned, kvg, wg, dense, terms, part, total,
    send1, recv1, send2, recv2, zsend1, zrecv1, zsend2, zrecv2,
    local_sem, kv_send, kv_recv, w_send, w_recv, rs_send, rs_recv, z_send, z_recv,
):
    rep = lax.axis_index("replica")
    shard = lax.axis_index("fsdp")
    band = lax.axis_index("tensor")
    tokens, width = x_in.shape
    side = terms.shape[-1]
    cap = weights.shape[1]
    cols = kv_grad.shape[1]
    hc = cap // 2
    ring = 4
    rows, groups = width // side, 8
    col_blocks = cols // side * groups
    piece = tokens // PIECES

    def shift(f, axis, by):
        y, x = f // ring, f % ring
        if axis == "x":
            return y * ring + (x + by + ring) % ring
        return ((y + by + ring) % ring) * ring + x

    def near(axis, by):
        return {"fsdp": shift(shard, axis, by)}

    def band_at(by):
        return (band + 2 * by + groups) % groups

    sibling = band + 1 - 2 * (band % 2)

    def sibling_at(by):
        return (sibling + 2 * by + groups) % groups

    def remote(src, dst, send_sem, recv_sem, where):
        return pltpu.make_async_remote_copy(
            src_ref=src, dst_ref=dst, send_sem=send_sem, recv_sem=recv_sem,
            device_id=where, device_id_type=MESH,
        )

    partners = [{"tensor": sibling}, {"tensor": band_at(1)}, {"tensor": band_at(-1)}]
    partners += [near(axis, by) for axis in ("x", "y") for by in (1, -1, 2)]
    partners += [{"replica": (rep + d) % 4} for d in (1, 2, 3)]
    barrier = pltpu.get_barrier_semaphore()
    for where in partners:
        pl.semaphore_signal(barrier, inc=1, device_id=where, device_id_type=MESH)
    pl.semaphore_wait(barrier, len(partners))

    sent = []

    def go(copy):
        copy.start()
        sent.append(copy)

    def kv_at(b, p, n=1):
        return kvg.at[b, pl.ds(p * piece, n * piece), :]

    own_kv = [kv_grad.at[pl.ds(p * piece, piece), :] for p in range(PIECES)]
    right_order = list(range(PIECES))
    left_order = right_order[PIECES // 2:] + right_order[:PIECES // 2]
    for a, b in zip(right_order, left_order):
        go(remote(own_kv[a], kv_at(band, a), kv_send.at[0, a], kv_recv.at[0, a], {"tensor": band_at(1)}))
        go(remote(own_kv[b], kv_at(band, b), kv_send.at[1, b], kv_recv.at[1, b], {"tensor": band_at(-1)}))

    firsts = ("x", "y")
    seconds = ("y", "x")

    def w_at(f, slot, n):
        return wg.at[pl.ds(f * cap + slot, n)]

    for h in range(2):
        own_w = weights.at[0, pl.ds(hc * h, hc)]
        for d, by in ((0, 1), (1, -1)):
            go(remote(own_w, w_at(shard, hc * h, hc), w_send.at[h, 0, d], w_recv.at[h, 0, d], near(firsts[h], by)))
            go(remote(own_w, w_at(shard, hc * h, hc), w_send.at[h, 2, d], w_recv.at[h, 2, d], near(seconds[h], by)))
    go(remote(kv_grad, kv_at(band, 0, PIECES), kv_send.at[3, 0], kv_recv.at[3, 0], {"tensor": sibling}))
    local = [
        pltpu.make_async_copy(inputs, x_in, local_sem.at[0]),
        pltpu.make_async_copy(kv_grad, kvg.at[band], local_sem.at[1]),
        pltpu.make_async_copy(weights.at[0], w_at(shard, 0, cap), local_sem.at[2]),
        pltpu.make_async_copy(bitmap, bits_in, local_sem.at[3]),
        pltpu.make_async_copy(counts, counts_in, local_sem.at[4]),
    ]
    for copy in local:
        copy.start()

    def kv_wait(which, p, b, n=1):
        remote(kv_at(b, p, n), kv_at(b, p, n), kv_send.at[which, p], kv_recv.at[which, p], {"tensor": sibling}).wait_recv()

    def kv_pass(which, p, b):
        go(remote(kv_at(b, p), kv_at(b, p), kv_send.at[which, p], kv_recv.at[which, p], {"tensor": sibling}))

    def kv_relay(p, b, by):
        go(remote(kv_at(b, p), kv_at(b, p), kv_send.at[2, p], kv_recv.at[2, p], {"tensor": band_at(by)}))

    def w_wait(h, which, d, f, slot, n):
        at = w_at(f, hc * h + slot, n)
        remote(at, at, w_send.at[h, which, d], w_recv.at[h, which, d], {"tensor": sibling}).wait_recv()

    def w_go(h, which, d, f, slot, n, axis):
        at = w_at(f, hc * h + slot, n)
        go(remote(at, at, w_send.at[h, which, d], w_recv.at[h, which, d], near(axis, 1 if d == 0 else -1)))

    hq = hc // 2

    def w_first(h):
        for d, by in ((0, -1), (1, 1)):
            src = shift(shard, firsts[h], by)
            w_wait(h, 0, d, src, 0, hc)
            w_go(h, 1, d, src, d * hq, hq, firsts[h])
            for e in range(2):
                w_go(h, 3 + d, e, src, 0, hc, seconds[h])

    def w_far(h):
        src = shift(shard, firsts[h], 2)
        for d in range(2):
            w_wait(h, 1, d, src, d * hq, hq)
        for e in range(2):
            w_go(h, 5, e, src, 0, hc, seconds[h])

    def w_second(h, s):
        for d, by in ((0, -1), (1, 1)):
            src = shift(shift(shard, firsts[h], (0, -1, 1, 2)[s]), seconds[h], by)
            w_wait(h, 2 + s, d, src, 0, hc)
            w_go(h, 6 + s, d, src, d * hq, hq, seconds[h])

    def w_last(h, s):
        src = shift(shift(shard, firsts[h], (0, -1, 1, 2)[s]), seconds[h], 2)
        for d in range(2):
            w_wait(h, 6 + s, d, src, d * hq, hq)

    def outer(b):
        def tile(i, carry):
            at = pl.ds(pl.multiple_of(i * 2 * side, 2 * side), 2 * side)
            got = jnp.dot(x_turned[at, :], kvg[b], preferred_element_type=jnp.float32)
            for u in range(2):
                for v in range(2):
                    place = (2 * i + u) * col_blocks + 2 * b + v
                    terms[place] = got[u * side:(u + 1) * side, v * side:(v + 1) * side]
            return carry

        lax.fori_loop(0, rows // 2, tile, 0)

    local[3].wait()
    local[4].wait()
    tables[...] = number(bits_in[...], counts_in[...], cap)
    to_scalars = pltpu.make_async_copy(tables, table, local_sem.at[5])
    to_scalars.start()
    local[0].wait()
    local[1].wait()
    x_turned[...] = x_in[...].T
    for h in range(2):
        w_first(h)
    outer(band)
    to_scalars.wait()
    for p, q in ((0, 2), (1, 3)):
        kv_wait(0, p, band_at(-1))
        kv_relay(p, band_at(-1), 1)
        kv_wait(1, q, band_at(1))
        kv_relay(q, band_at(1), -1)
        kv_pass(4, p, band_at(-1))
        kv_pass(5, q, band_at(1))
        if p == 0:
            for h in range(2):
                w_far(h)
            for h in range(2):
                w_second(h, 0)
            kv_wait(3, 0, sibling, PIECES)
            outer(sibling)
    for s in range(1, 4):
        for h in range(2):
            w_second(h, s)
    for p, q in ((2, 0), (3, 1)):
        kv_wait(0, p, band_at(-1))
        kv_pass(4, p, band_at(-1))
        kv_wait(1, q, band_at(1))
        kv_pass(5, q, band_at(1))
    outer(band_at(-1))
    outer(band_at(1))
    for p in range(PIECES):
        kv_wait(4, p, sibling_at(-1))
        kv_wait(5, p, sibling_at(1))
    outer(sibling_at(-1))
    outer(sibling_at(1))
    for h in range(2):
        for s in range(4):
            w_last(h, s)
    local[2].wait()
    wg[wg.shape[0] - 1] = jnp.zeros((side, side), wg.dtype)

    def fill(i, carry):
        for j in range(col_blocks):
            place = i * col_blocks + j
            dense[pl.ds(pl.multiple_of(i * side, side), side), j * side:(j + 1) * side] = wg[jnp.clip(table[1, place], 0, wg.shape[0] - 1)]
        return carry

    lax.fori_loop(0, rows, fill, 0)
    for p in (0, 2, 1, 3):
        kv_wait(2, p, band_at(2))
        kv_pass(6, p, band_at(2))
    outer(band_at(2))
    for p in (0, 2, 1, 3):
        kv_wait(6, p, sibling_at(2))
    outer(sibling_at(2))

    n1 = ring * hq

    def coord(axis):
        return shard % ring if axis == "x" else shard // ring

    def owner(h, one, two):
        return two * ring + one if firsts[h] == "x" else one * ring + two

    def term1(w, h, one, k, upper):
        slot = owner(h, one, k // hq) * cap + hc * h + upper * hq + k % hq
        return terms[jnp.clip(table[0, slot], 0, terms.shape[0] - 1), pl.ds(WAVES[w][0], WAVES[w][1]), :]

    def tall(w, blocks):
        return pl.ds(0, blocks * WAVES[w][1] // 2 + 8)

    def own_part(w, h, two, upper, k):
        return part[w, h, two * hc + upper * hq + k, pl.ds(0, WAVES[w][1]), :]

    kinds = {M_R: (2, 0, 1), M_L: (2, 1, -1), O_R: (1, 1, 1), O_L: (-1, 0, -1), C_R: (1, 0, 1), C_L: (-1, 1, -1)}

    def rs_copy(phase, w, h, kind):
        axis = (firsts if phase == 0 else seconds)[h]
        src, dst = ((send1, recv1), (send2, recv2))[phase]
        blocks = (n1, hq)[phase]
        return remote(
            src.at[w, h, kind, tall(w, blocks)], dst.at[w, h, kind, tall(w, blocks)], rs_send.at[phase, w, h, kind], rs_recv.at[phase, w, h, kind],
            near(axis, kinds[kind][0] if phase == 1 else kinds[kind][2]),
        )

    def first_send(w, pair):
        for kind in pair:
            for h in range(2):
                by, upper, _ = kinds[kind]
                one = (coord(firsts[h]) + by + ring) % ring
                relayed = {C_R: M_R, C_L: M_L}.get(kind)
                if relayed is not None:
                    rs_copy(0, w, h, relayed).wait_recv()

                for k in range(n1):
                    value = term1(w, h, one, k, upper)
                    if relayed is not None:
                        value = value + decode(recv1.at[w, h, relayed], n1, k, WAVES[w][1])
                    encode(send1.at[w, h, kind], n1, k, value)
                go(rs_copy(0, w, h, kind))

    def first_sum(w):
        for h in range(2):
            for kind in (O_R, O_L, C_R, C_L):
                rs_copy(0, w, h, kind).wait_recv()
            one = coord(firsts[h])

            for k in range(n1):
                for upper, pair in ((0, (C_R, O_L)), (1, (C_L, O_R))):
                    value = term1(w, h, one, k, upper)
                    for kind in pair:
                        value = value + decode(recv1.at[w, h, kind], n1, k, WAVES[w][1])
                    part[w, h, (k // hq) * hc + upper * hq + k % hq, pl.ds(0, WAVES[w][1]), :] = value

    def second_send(w):
        for h in range(2):
            for kind in range(6):
                by, upper, _ = kinds[kind]
                two = (coord(seconds[h]) + by + ring) % ring
                for k in range(hq):
                    encode(send2.at[w, h, kind], hq, k, own_part(w, h, two, upper, k))
            for kind in range(6):
                go(rs_copy(1, w, h, kind))

    def second_sum(w):
        for h in range(2):
            for kind in range(6):
                rs_copy(1, w, h, kind).wait_recv()
        for h in range(2):
            two = coord(seconds[h])
            for upper, three in ((0, (C_R, O_L, M_R)), (1, (C_L, O_R, M_L))):
                for k in range(hq):
                    value = own_part(w, h, two, upper, k)
                    for kind in three:
                        value = value + decode(recv2.at[w, h, kind], hq, k, WAVES[w][1])
                    total[hc * h + upper * hq + k, pl.ds(WAVES[w][0], WAVES[w][1]), :] = value

    zq = cap // 4

    def z_copy(phase, w, d):
        src = zsend1.at[w, d - 1, tall(w, zq)] if phase == 0 else zsend2.at[w, tall(w, zq)]
        dst = (zrecv1, zrecv2)[phase].at[w, d - 1, tall(w, zq)]
        return remote(src, dst, z_send.at[phase, w, d - 1], z_recv.at[phase, w, d - 1], {"replica": (rep + d) % 4})

    def summed(w, who, k):
        return total[who * zq + k, pl.ds(WAVES[w][0], WAVES[w][1]), :]

    def z_scatter(w):
        for d in (2, 1, 3):
            for k in range(zq):
                encode(zsend1.at[w, d - 1], zq, k, summed(w, (rep + d) % 4, k))
        for d in (2, 1, 3):
            go(z_copy(0, w, d))

    def put(buf, w, who):
        for k in range(zq):
            slot = who * zq + k
            value = decode(buf, zq, k, WAVES[w][1])
            weight_grad[0, slot, pl.ds(WAVES[w][0], WAVES[w][1]), :] = jnp.where(slot < shard_counts[0, shard], value, 0.0)

    def z_hand(w):
        for d in (1, 3, 2):
            z_copy(0, w, d).wait_recv()
        for k in range(zq):
            value = summed(w, rep, k)
            for d in (1, 3, 2):
                value = value + decode(zrecv1.at[w, d - 1], zq, k, WAVES[w][1])
            encode(zsend2.at[w], zq, k, value)
        for d in (2, 1, 3):
            go(z_copy(1, w, d))
        put(zsend2.at[w], w, rep)

    def z_take(w):
        for d in (1, 3, 2):
            z_copy(1, w, d).wait_recv()
        for d in (1, 3, 2):
            put(zrecv2.at[w, d - 1], w, (rep - d + 4) % 4)

    def product(i, carry):
        at = pl.ds(pl.multiple_of(i * 2 * side, 2 * side), 2 * side)
        acc = jnp.zeros((tokens, 2 * side), jnp.float32)
        for b in range(groups):
            acc = acc + lax.dot_general(
                kvg[b], dense[at, b * cols:(b + 1) * cols], (((1,), (1,)), ((), ())),
                preferred_element_type=jnp.float32,
            )
        input_grad[:, at] = acc.astype(input_grad.dtype)
        return carry

    early, alone, late = (M_R, M_L), (O_R, O_L), (C_R, C_L)
    first_send(0, early)
    first_send(0, alone)
    first_send(0, late)
    first_send(1, early)
    first_send(1, alone)
    lax.fori_loop(0, rows // 2, product, 0)
    first_sum(0)
    second_send(0)
    first_send(1, late)
    second_sum(0)
    z_scatter(0)
    first_sum(1)
    second_send(1)
    z_hand(0)
    second_sum(1)
    over = len(sent)
    z_scatter(1)
    for copy in sent[:over]:
        copy.wait_send()
    del sent[:over]
    z_take(0)
    z_hand(1)
    z_take(1)
    for copy in sent:
        copy.wait_send()


def body(inputs, kv_grad, weight_blocks, bitmap, counts):
    side = weight_blocks.shape[-1]
    cap = weight_blocks.shape[1]
    shards = counts.shape[1]
    slots = shards * cap
    tokens, width = inputs.shape
    cols = kv_grad.shape[1]
    places = bitmap.size
    groups = 8
    waves, half = len(WAVES), max(n for _, n in WAVES) // 2
    big, small = cap * half + 8, cap // 4 * half + 8
    held = pl.BlockSpec(memory_space=pltpu.HBM)
    fast = pl.BlockSpec(memory_space=pltpu.VMEM)
    scalars = pl.BlockSpec(memory_space=pltpu.SMEM)
    return pl.pallas_call(
        kernel,
        out_shape=(
            jax.ShapeDtypeStruct(inputs.shape, jnp.bfloat16),
            jax.ShapeDtypeStruct(weight_blocks.shape, jnp.float32),
        ),
        in_specs=[scalars, held, held, held, held, held],
        out_specs=(fast, fast),
        scratch_shapes=[
            pltpu.VMEM(bitmap.shape, jnp.int32),
            pltpu.VMEM(counts.shape, jnp.int32),
            pltpu.VMEM((8, places), jnp.int32),
            pltpu.SMEM((8, places), jnp.int32),
            pltpu.VMEM((tokens, width), jnp.bfloat16),
            pltpu.VMEM((width, tokens), jnp.bfloat16),
            pltpu.VMEM((groups, tokens, cols), jnp.bfloat16),
            pltpu.VMEM((slots + 1, side, side), jnp.bfloat16),
            pltpu.VMEM((width, groups * cols), jnp.bfloat16),
            pltpu.VMEM((places, side, side), jnp.float32),
            pltpu.VMEM((waves, 2, 2 * cap, 2 * half, side), jnp.float32),
            pltpu.VMEM((cap, side, side), jnp.float32),
            pltpu.VMEM((waves, 2, 6, big, side), jnp.int32),
            pltpu.VMEM((waves, 2, 6, big, side), jnp.int32),
            pltpu.VMEM((waves, 2, 6, small, side), jnp.int32),
            pltpu.VMEM((waves, 2, 6, small, side), jnp.int32),
            pltpu.VMEM((waves, 3, small, side), jnp.int32),
            pltpu.VMEM((waves, 3, small, side), jnp.int32),
            pltpu.VMEM((waves, small, side), jnp.int32),
            pltpu.VMEM((waves, 3, small, side), jnp.int32),
            pltpu.SemaphoreType.DMA((6,)),
            pltpu.SemaphoreType.DMA((7, PIECES)),
            pltpu.SemaphoreType.DMA((7, PIECES)),
            pltpu.SemaphoreType.DMA((2, 10, 2)),
            pltpu.SemaphoreType.DMA((2, 10, 2)),
            pltpu.SemaphoreType.DMA((2, waves, 2, 6)),
            pltpu.SemaphoreType.DMA((2, waves, 2, 6)),
            pltpu.SemaphoreType.DMA((2, waves, 3)),
            pltpu.SemaphoreType.DMA((2, waves, 3)),
        ],
        compiler_params=pltpu.CompilerParams(
            collective_id=0, has_side_effects=True, vmem_limit_bytes=48 * 1024 * 1024
        ),
    )(counts, *(pltpu.with_memory_space_constraint(a, pltpu.HBM) for a in (inputs, kv_grad, weight_blocks, bitmap, counts)))


def solution(mesh):
    in_specs = (
        P(("replica", "fsdp"), "tensor"),
        P(("replica", "fsdp"), "tensor"),
        P("tensor", "fsdp", None, None),
        P("tensor", None),
        P("tensor", None),
    )
    out_specs = (P(("replica", "fsdp"), "tensor"), P("tensor", "fsdp", None, None))
    return jax.shard_map(body, mesh=mesh, in_specs=in_specs, out_specs=out_specs, check_vma=False)
```
